32 devices in a mesh: groups: 2 (over x), inst: 4 (over y, core), tp: 4 (over z).
Axes of the slice: x: 2, y: 2, z: 4, core: 2. Of those that a mesh axis runs over, the one named last changes fastest.
Arguments:
- queries: bfloat16 [512, 8192], P(('groups', 'inst'), 'tp'), parts along dimension 0, may hold values from -40 to 40
- k_pool: bfloat16 [1024, 8, 128, 128], P(('groups', 'inst'), 'tp'), parts along dimension 0, may hold values from -6 to 6
- v_pool: bfloat16 [1024, 8, 128, 128], P(('groups', 'inst'), 'tp'), parts along dimension 0, may hold values from -6 to 6
- out_weight: bfloat16 [8192, 4096], P('tp'), may hold values from -0.5 to 0.5
- lengths: int32 [8, 32], P(('groups', 'inst')), parts along dimension 0, may hold values from 1 to 512, 8192 in all within a row
- block_table: int32 [8, 128], P(('groups', 'inst')), parts along dimension 0, may hold values from 0 to 127, each once within a row
- routes: int32 [256, 1], P(('groups', 'inst')), parts along dimension 0, may hold values from 0 to 3; in each aligned block of 32 rows (0 to 31, 32 to 63, ...) at most 16 rows name the same one
Outputs:
- attended: bfloat16 [512, 4096], P(('groups', 'inst')), parts along dimension 0
The draws below stay inside these ranges and needn't reach their ends.
There are 2 independent parts, one for each index of `groups`. The reference program is written for one: setup_inputs(seed, part) draws one part's arguments, and reference() takes and returns one part's arrays. A program takes and returns all parts, laid end to end along the dimension named above; an argument that names none is the same for every part. Nothing has to cross between parts.
Inputs may be any that keep to these rules, and one draw needn't show every extreme that they name: `routes`: in the rows of one instance no target is named more than 16 times, a bound that some block reaches. The 32 lengths of each instance sum to 8192, and the largest is 512. `block_table`: each instance's row names each of its 128 pool blocks once.
All inputs are finite; a program needn't handle non-finite values.
Results may differ from the reference program's by a relative error of at most 0.0058.
Values may be sent and summed in bfloat16 or wider, within the bound.
A program may use at most 192 MiB of HBM per device.

```python
import math
import jax
import jax.numpy as jnp
import numpy as np
from jax import lax

D = 4096
KVH = 8
GROUP = 8
HD = 128
BLK = 128
MAXB = 4
ROWS = 32
CAP = 16
NBLK = 128
HEADS = 64
SLOTS = 64
N_INST = 4


def draw_k_pool(key, part):
    key = jax.random.fold_in(key, 3)
    shape = (N_INST * NBLK, KVH, BLK, HD)
    result = jnp.clip(jax.random.normal(key, shape, jnp.float32), -6.0, 6.0)
    return result.astype(jnp.bfloat16)


def draw_queries(key, part):
    key = jax.random.fold_in(key, 5)
    rows_all = N_INST * N_INST * CAP
    result = jnp.clip(jax.random.normal(key, (rows_all, KVH * GROUP * HD), jnp.float32), -6.0, 6.0)
    return result.astype(jnp.bfloat16)


def level_of(own_key, shape, pieces, low, top_value):
    gain, own = 1.0, jax.random.fold_in(own_key, 6)
    for dim, blocks in pieces:
        heights = jnp.exp(jax.random.uniform(jax.random.fold_in(own, dim), (blocks,), jnp.float32, low / len(pieces), top_value / len(pieces)))
        gain = gain * jnp.repeat(heights, shape[dim] // blocks).reshape([-1 if axis == dim else 1 for axis in range(len(shape))])
    return gain


def split_up(count, total, limit, lean):
    weights = [(1 << 20) // math.isqrt(rank ** lean) + 1 for rank in range(2, count + 1)]
    rest, counts = total - limit - (count - 1), [1] * (count - 1)
    while rest > 0:
        candidates = [i for i in range(count - 1) if counts[i] < limit]
        pool, remaining = sum([weights[i] for i in candidates]), rest
        for i in candidates:
            extra = min(limit - counts[i], max(1, remaining * weights[i] // pool), rest)
            counts[i] = counts[i] + extra
            rest = rest - extra
    return np.array([limit] + counts)


def uneven_parts(rng, amount, total, most, skew):
    if amount == 2:
        one = jax.random.randint(rng, (), max(1, total - most), min(most, total - 1) + 1)
        return jnp.stack([one, total - one])
    sizes = jnp.asarray(split_up(amount, total, most, skew), jnp.int32)
    twos = (amount - 1) // 2
    source_of, receiver = sizes[1:1 + 2 * twos:2], sizes[2:2 + 2 * twos:2]
    room = jnp.minimum(source_of - 1, most - receiver)
    passed = jax.random.randint(jax.random.fold_in(rng, 1), (twos,), 0, 1 << 20) % (room + 1)
    sizes = sizes.at[1:1 + 2 * twos:2].set(source_of - passed).at[2:2 + 2 * twos:2].set(receiver + passed)
    return sizes[jax.random.permutation(jax.random.fold_in(rng, 2), amount)]


def shared_out(key, own, number, rows, amount, top, bound, skew):
    order = jax.random.permutation(key, amount)
    crowded, common = shares(amount, rows * top, bound, skew, True), shares(amount, rows * top, bound, skew, False)
    places = jnp.arange(amount)

    def named(tallies, rotation):
        used = int((tallies > 0).sum())
        fixed = max(1, used // 4)
        passed = fixed + (places - fixed + rotation * (used - fixed)) % max(1, amount - fixed)
        return jnp.zeros((amount,), jnp.int32).at[order[jnp.where(places < fixed, places, passed)]].set(jnp.asarray(tallies, jnp.int32))

    tallies = jnp.where(number % 4 == 0, named(crowded, number // 4), named(common, number - number // 4 - 1))
    mixed = jax.random.permutation(jax.random.fold_in(own, 3), amount)
    giver, taker = mixed[0:amount // 2 * 2:2], mixed[1:amount // 2 * 2:2]
    slack = jnp.minimum(tallies[giver] - 1, bound - tallies[taker]) // 2
    slack = jnp.where((giver == order[0]) | (taker == order[0]) | (tallies[taker] == 0), 0, jnp.maximum(slack, 0))
    passed = jax.random.randint(jax.random.fold_in(own, 4), (amount // 2,), 0, 1 << 20) % (slack + 1)
    tallies = tallies.at[giver].add(-passed).at[taker].add(passed)
    items = jnp.searchsorted(jnp.cumsum(tallies), jnp.arange(rows * top), side="right").astype(jnp.int32)
    table = items.reshape(top, rows).T
    table = table[jax.random.permutation(jax.random.fold_in(own, 1), rows)]
    rotation = jax.random.randint(jax.random.fold_in(own, 2), (rows, 1), 0, top)
    return jnp.take_along_axis(table, (jnp.arange(top)[None, :] + rotation) % top, axis=1)


def shares(amount, total, bound, slope, full):
    portions = [(1 << 20) // math.isqrt(standing ** slope) + 1 for standing in range(1, amount + 1)]
    largest = bound if full else min(bound, max(-(-total // amount), total * portions[0] // sum(portions)))
    least = 1 if total - largest >= amount - 1 else 0
    given, surplus = [largest] + [least] * (amount - 1), total - largest - least * (amount - 1)
    while surplus > 0:
        movable = [i for i in range(1, amount) if given[i] < largest] or [i for i in range(1, amount) if given[i] < bound]
        pool, left = sum([portions[i] for i in movable]), surplus
        for i in movable:
            addition = min(bound - given[i], max(1, left * portions[i] // pool), surplus)
            given[i] = given[i] + addition
            surplus = surplus - addition
    return np.array(given)


def scatter_about(rng, extent, scale, limit, cuts=(), kind=jnp.bfloat16):
    level = level_of(rng, extent, cuts, -0.22, 0.18) if cuts else 1.0
    array = jax.random.normal(rng, extent, jnp.float32) * scale * level
    return jnp.minimum(jnp.maximum(array, -limit), limit).astype(kind)


def setup_inputs(seed: int = 0, part: int = 0) -> dict:
    arg_keys = jax.random.split(jax.random.key(seed), 8)
    part_splits = jax.random.split(jax.random.fold_in(arg_keys[7], part), 8)
    queries = draw_queries(jax.random.fold_in(jax.random.fold_in(arg_keys[7], part), 71), part)
    k_pool = draw_k_pool(jax.random.fold_in(jax.random.fold_in(arg_keys[7], part), 71), part)
    v_pool = scatter_about(part_splits[2], (N_INST * NBLK, KVH, BLK, HD), 1.0, 6.0, ((0, 4), (1, 4)))
    out_weight = scatter_about(arg_keys[3], (HEADS * HD, D), (HEADS * HD // 64) ** -0.5, 0.5, ((0, 4),))
    lengths = jax.vmap(lambda own: uneven_parts(own, ROWS, ROWS * MAXB * BLK // 2, MAXB * BLK, 2))(jax.random.split(part_splits[4], N_INST)).reshape((N_INST, ROWS)).astype(jnp.int32)
    block_table = jax.vmap(lambda own: jax.random.permutation(own, NBLK))(jax.random.split(part_splits[5], N_INST)).reshape((N_INST, NBLK)).astype(jnp.int32)
    routes_keys = jax.random.split(jax.random.fold_in(part_splits[6], 1), (N_INST * ROWS) // ROWS)
    routes_turns = jax.random.permutation(jax.random.fold_in(part_splits[6], 3), (N_INST * ROWS) // ROWS)
    routes = jax.vmap(lambda own, number: shared_out(jax.random.fold_in(part_splits[6], 2), own, number, ROWS, N_INST, 1, CAP, 2))(routes_keys, routes_turns).reshape((N_INST * ROWS, 1))
    return dict(queries=queries, k_pool=k_pool, v_pool=v_pool, out_weight=out_weight, lengths=lengths, block_table=block_table, routes=routes)


def attend(query, key_rows, value_rows, ctx_len):
    slots = query.shape[0]
    head_dim = key_rows.shape[4]
    grouped = query.astype(jnp.float32).reshape(slots, key_rows.shape[2], -1, head_dim)
    scores = jnp.einsum('skgd,smkbd->skgmb', grouped, key_rows.astype(jnp.float32)) / math.sqrt(head_dim)
    position = jnp.arange(key_rows.shape[1] * key_rows.shape[3], dtype=jnp.int32).reshape(key_rows.shape[1], key_rows.shape[3])
    visible = (position[None] < ctx_len[:, None, None])[:, None, None]
    scores = jnp.where(visible, scores, -1e+30)
    peak = lax.optimization_barrier(jnp.max(scores, axis=(3, 4), keepdims=True))
    scaled = jnp.exp(scores - peak)
    weights = (scaled / lax.optimization_barrier(jnp.sum(scaled, axis=(3, 4), keepdims=True))).astype(jnp.bfloat16)
    mixed = jnp.einsum('skgmb,smkbd->skgd', weights.astype(jnp.float32), value_rows.astype(jnp.float32)).astype(jnp.bfloat16)
    mixed = jnp.where((ctx_len > 0)[:, None, None, None], mixed, jnp.zeros_like(mixed))
    return mixed.reshape(slots, -1)

def reference(queries, k_pool, v_pool, out_weight, lengths, block_table, routes):
    target = routes[:, 0].reshape(N_INST, ROWS)
    onehot = (target[:, :, None] == jnp.arange(N_INST, dtype=jnp.int32)[None, None, :]).astype(jnp.int32)
    before = jnp.cumsum(onehot, axis=1) - onehot
    rank_in = lax.optimization_barrier(jnp.sum(before * onehot, axis=2))
    slot_index = target * SLOTS + jnp.arange(N_INST, dtype=jnp.int32)[:, None] * CAP + rank_in
    source = jnp.full((N_INST * SLOTS,), -1, jnp.int32).at[slot_index.reshape(-1)].set(jnp.arange(N_INST * ROWS, dtype=jnp.int32))
    filled = source >= 0
    anchor = jnp.maximum(source, 0)
    ctx_len = jnp.where(filled, lengths.reshape(-1)[anchor], 0).astype(jnp.int32)
    block_ids = block_table.reshape(N_INST * ROWS, MAXB)[anchor] + (anchor // ROWS * NBLK)[:, None]
    block_ids = block_ids.astype(jnp.int32)

    def per_instance(items):
        query, chosen, spans = items
        head_out = attend(query, k_pool[chosen], v_pool[chosen], spans)
        return jnp.dot(head_out, out_weight, preferred_element_type=jnp.float32).astype(jnp.bfloat16)
    result = lax.map(per_instance, (queries.reshape(N_INST, SLOTS, -1), block_ids.reshape(N_INST, SLOTS, MAXB), ctx_len.reshape(N_INST, SLOTS)))
    return result.reshape(N_INST * SLOTS, D)
```

```python
import functools
import math

import jax
import jax.numpy as jnp
from jax import lax
from jax.experimental import pallas as pl
from jax.experimental.pallas import tpu as pltpu
from jax.sharding import PartitionSpec as P

MESH = pl.DeviceIdType.MESH
F32 = jnp.float32
BF16 = jnp.bfloat16
PIECES = 4


def kernel(
    num_inst, num_tp, q_hbm, k_hbm, v_hbm, w_hbm, len_ref, table_ref, route_ref, out_ref,
    k_buf, v_buf, w_buf, q_in, q_heads, score, mixed, act, place_t, rs_send, rs_in, own, gathered, y_send,
    k_sem, v_sem, w_sem, q_own_sem, q_ssem, q_rsem, rs_ssem, rs_rsem, ag_ssem, ag_rsem, y_ssem, y_rsem,
):
    me = lax.axis_index("inst")
    tp = lax.axis_index("tp")
    blocks, kv_heads, block_len, head_dim = k_buf.shape
    cap = q_in.shape[1]
    cols = q_in.shape[2]
    rows = route_ref.shape[0]
    heads = cols // head_dim
    group = heads // kv_heads
    per_req = table_ref.shape[1] // rows
    chunk = w_buf.shape[2]

    def inst_peer(k):
        return lax.rem(me + k, num_inst)

    def tp_peer(k):
        return lax.rem(tp + k, num_tp)

    size = blocks // PIECES
    k_copies = [
        pltpu.make_async_copy(k_hbm.at[pl.ds(i * size, size)], k_buf.at[pl.ds(i * size, size)], k_sem.at[i])
        for i in range(PIECES)
    ]
    v_copies = [
        pltpu.make_async_copy(v_hbm.at[pl.ds(i * size, size)], v_buf.at[pl.ds(i * size, size)], v_sem.at[i])
        for i in range(PIECES)
    ]
    w_copies = []
    for i in range(num_tp):
        column = pl.multiple_of(tp_peer((i + 1) % num_tp) * chunk, 128)
        w_copies.append(pltpu.make_async_copy(w_hbm.at[:, pl.ds(column, chunk)], w_buf.at[i], w_sem.at[i]))
    q_own = pltpu.make_async_copy(q_hbm.at[me], q_in.at[me], q_own_sem)
    q_own.start()
    for c in k_copies + v_copies + w_copies:
        c.start()

    barrier = pltpu.get_barrier_semaphore()
    for k in range(1, num_inst):
        pl.semaphore_signal(barrier, inc=1, device_id={"inst": inst_peer(k)}, device_id_type=MESH)
    for k in range(1, num_tp):
        pl.semaphore_signal(barrier, inc=1, device_id={"tp": tp_peer(k)}, device_id_type=MESH)
    pl.semaphore_wait(barrier, num_inst + num_tp - 2)

    q_copies = []
    for k in range(1, num_inst):
        peer = inst_peer(k)
        c = pltpu.make_async_remote_copy(
            src_ref=q_hbm.at[peer], dst_ref=q_in.at[me], send_sem=q_ssem.at[k], recv_sem=q_rsem.at[me],
            device_id={"inst": peer}, device_id_type=MESH,
        )
        c.start()
        q_copies.append(c)

    target = route_ref[...]
    lane = lax.broadcasted_iota(jnp.int32, (rows, 128), 1)
    onehot = (target == lane).astype(F32)
    earlier = (
        lax.broadcasted_iota(jnp.int32, (rows, rows), 0) > lax.broadcasted_iota(jnp.int32, (rows, rows), 1)
    ).astype(F32)
    before = jnp.dot(earlier, onehot, preferred_element_type=F32)
    rank = jnp.sum(before * onehot, axis=1, keepdims=True).astype(jnp.int32)
    slot = target * cap + rank
    place = (slot == lane).astype(F32)
    turned = jnp.transpose(place)
    for t in range(num_inst):
        place_t[t] = turned[t * cap:(t + 1) * cap, :]

    q_own.wait()
    for k in range(1, num_inst):
        src = inst_peer(k)
        pltpu.make_async_remote_copy(
            src_ref=q_hbm.at[src], dst_ref=q_in.at[src], send_sem=q_ssem.at[k], recv_sem=q_rsem.at[src],
            device_id={"inst": src}, device_id_type=MESH,
        ).wait_recv()
    total = jnp.zeros((rows, cols), F32)
    for t in range(num_inst):
        here = (slot - t * cap == lax.broadcasted_iota(jnp.int32, (rows, cap), 1)).astype(F32).astype(BF16)
        total = total + jnp.dot(here, q_in[t], preferred_element_type=F32)
    for h in range(heads):
        q_heads[:, h, :] = total[:, h * head_dim:(h + 1) * head_dim]

    for c in k_copies:
        c.wait()
    span = per_req * block_len
    position = lax.broadcasted_iota(jnp.int32, (group, span), 1)
    scale = 1.0 / math.sqrt(head_dim)

    def score_step(i, carry):
        for u in range(4):
            r = i * 4 + u
            limit = len_ref[0, r]
            ids = [table_ref[0, r * per_req + m] for m in range(per_req)]
            for j in range(kv_heads):
                query = q_heads[r, pl.ds(j * group, group), :].astype(BF16)
                keys = jnp.concatenate([k_buf[b, j] for b in ids], axis=0)
                s = lax.dot_general(query, keys, (((1,), (1,)), ((), ())), preferred_element_type=F32) * scale
                score[r, pl.ds(j * group, group), :] = jnp.where(position < limit, s, -1e30)
        return carry

    lax.fori_loop(0, rows // 4, score_step, 0)

    def soft_step(i, carry):
        x = score[pl.ds(i * 4, 4)]
        e = jnp.exp(x - jnp.max(x, axis=2, keepdims=True))
        score[pl.ds(i * 4, 4)] = e / jnp.sum(e, axis=2, keepdims=True)
        return carry

    lax.fori_loop(0, rows // 4, soft_step, 0)

    for c in v_copies:
        c.wait()

    def mix_step(i, carry):
        for u in range(4):
            r = i * 4 + u
            ids = [table_ref[0, r * per_req + m] for m in range(per_req)]
            for j in range(kv_heads):
                weight = score[r, pl.ds(j * group, group), :].astype(BF16)
                values = jnp.concatenate([v_buf[b, j] for b in ids], axis=0)
                mixed[r, pl.ds(j * group, group), :] = jnp.dot(weight, values, preferred_element_type=F32)
        return carry

    lax.fori_loop(0, rows // 4, mix_step, 0)
    for h in range(heads):
        act[:, h * head_dim:(h + 1) * head_dim] = mixed[:, h, :].astype(BF16)

    tile = min(256, chunk)
    rs_copies = []
    for i in range(num_tp):
        w_copies[i].wait()

        def project(n, carry, i=i):
            column = pl.ds(pl.multiple_of(n * tile, tile), tile)
            part = jnp.dot(act[...], w_buf[i, :, column], preferred_element_type=F32)
            if i < num_tp - 1:
                rs_send[i, :, column] = part.astype(BF16)
            else:
                own[:, column] = part
            return carry

        lax.fori_loop(0, chunk // tile, project, 0)
        if i < num_tp - 1:
            c = pltpu.make_async_remote_copy(
                src_ref=rs_send.at[i], dst_ref=rs_in.at[tp], send_sem=rs_ssem.at[i], recv_sem=rs_rsem.at[tp],
                device_id={"tp": tp_peer(i + 1)}, device_id_type=MESH,
            )
            c.start()
            rs_copies.append(c)

    summed = own[...]
    for k in range(1, num_tp):
        src = tp_peer(k)
        pltpu.make_async_remote_copy(
            src_ref=rs_send.at[0], dst_ref=rs_in.at[src], send_sem=rs_ssem.at[0], recv_sem=rs_rsem.at[src],
            device_id={"tp": src}, device_id_type=MESH,
        ).wait_recv()
        summed = summed + rs_in[src].astype(F32)
    gathered[tp] = summed.astype(BF16)

    ag_copies = []
    for k in range(1, num_tp):
        c = pltpu.make_async_remote_copy(
            src_ref=gathered.at[tp], dst_ref=gathered.at[tp], send_sem=ag_ssem.at[k], recv_sem=ag_rsem.at[tp],
            device_id={"tp": tp_peer(k)}, device_id_type=MESH,
        )
        c.start()
        ag_copies.append(c)

    y_copies = []
    for k in range(num_tp):
        src = tp_peer(k)
        if k:
            pltpu.make_async_remote_copy(
                src_ref=gathered.at[src], dst_ref=gathered.at[src], send_sem=ag_ssem.at[k], recv_sem=ag_rsem.at[src],
                device_id={"tp": src}, device_id_type=MESH,
            ).wait_recv()
        column = pl.ds(pl.multiple_of(src * chunk, 128), chunk)
        block = gathered[src]
        for n in list(range(1, num_inst)) + [0]:
            dst = inst_peer(n)
            moved = jnp.dot(place_t[dst].astype(BF16), block, preferred_element_type=F32).astype(BF16)
            if n == 0:
                out_ref[me, :, column] = moved
                continue
            y_send[k, n] = moved
            c = pltpu.make_async_remote_copy(
                src_ref=y_send.at[k, n], dst_ref=out_ref.at[me, :, column],
                send_sem=y_ssem.at[k, n], recv_sem=y_rsem.at[src, me],
                device_id={"inst": dst}, device_id_type=MESH,
            )
            c.start()
            y_copies.append(c)

    for k in range(num_tp):
        piece = tp_peer(k)
        column = pl.ds(pl.multiple_of(piece * chunk, 128), chunk)
        for n in range(1, num_inst):
            src = inst_peer(n)
            pltpu.make_async_remote_copy(
                src_ref=y_send.at[k, n], dst_ref=out_ref.at[src, :, column],
                send_sem=y_ssem.at[k, n], recv_sem=y_rsem.at[piece, src],
                device_id={"inst": src}, device_id_type=MESH,
            ).wait_recv()
    for c in q_copies + rs_copies + ag_copies + y_copies:
        c.wait_send()


def local(queries, k_pool, v_pool, out_weight, lengths, block_table, routes):
    num_inst = lax.axis_size("inst")
    num_tp = lax.axis_size("tp")
    slots, cols = queries.shape
    cap = slots // num_inst
    blocks, kv_heads, block_len, head_dim = k_pool.shape
    rows = routes.shape[0]
    features = out_weight.shape[1]
    chunk = features // num_tp
    heads = cols // head_dim
    span = block_table.shape[1] // rows * block_len
    anywhere = pl.BlockSpec(memory_space=pl.ANY)
    smem = pl.BlockSpec(memory_space=pltpu.SMEM)
    vmem = pl.BlockSpec(memory_space=pltpu.VMEM)
    dma = pltpu.SemaphoreType.DMA
    out = pl.pallas_call(
        functools.partial(kernel, num_inst, num_tp),
        out_shape=jax.ShapeDtypeStruct((num_inst, cap, features), BF16),
        in_specs=[anywhere, anywhere, anywhere, anywhere, smem, smem, vmem],
        out_specs=vmem,
        scratch_shapes=[
            pltpu.VMEM(k_pool.shape, BF16),
            pltpu.VMEM(v_pool.shape, BF16),
            pltpu.VMEM((num_tp, cols, chunk), BF16),
            pltpu.VMEM((num_inst, cap, cols), BF16),
            pltpu.VMEM((rows, heads, head_dim), F32),
            pltpu.VMEM((rows, heads, span), F32),
            pltpu.VMEM((rows, heads, head_dim), F32),
            pltpu.VMEM((rows, cols), BF16),
            pltpu.VMEM((num_inst, cap, rows), F32),
            pltpu.VMEM((num_tp, rows, chunk), BF16),
            pltpu.VMEM((num_tp, rows, chunk), BF16),
            pltpu.VMEM((rows, chunk), F32),
            pltpu.VMEM((num_tp, rows, chunk), BF16),
            pltpu.VMEM((num_tp, num_inst, cap, chunk), BF16),
            dma((PIECES,)),
            dma((PIECES,)),
            dma((num_tp,)),
            dma,
            dma((num_inst,)),
            dma((num_inst,)),
            dma((num_tp,)),
            dma((num_tp,)),
            dma((num_tp,)),
            dma((num_tp,)),
            dma((num_tp, num_inst)),
            dma((num_tp, num_inst)),
        ],
        compiler_params=pltpu.CompilerParams(
            collective_id=0, has_side_effects=True, vmem_limit_bytes=48 * 1024 * 1024
        ),
        cost_estimate=pl.CostEstimate(flops=10**9, bytes_accessed=33 * 10**6, transcendentals=300000),
    )(queries.reshape(num_inst, cap, cols), k_pool, v_pool, out_weight, lengths, block_table, routes)
    return out.reshape(slots, features)


def solution(mesh):
    return jax.shard_map(
        local,
        mesh=mesh,
        in_specs=(
            P(("groups", "inst"), "tp"),
            P(("groups", "inst"), "tp", None, None),
            P(("groups", "inst"), "tp", None, None),
            P("tp", None),
            P(("groups", "inst"), None),
            P(("groups", "inst"), None),
            P(("groups", "inst"), None),
        ),
        out_specs=P(("groups", "inst"), None),
        check_vma=False,
    )
```

```python
import functools
import math

import jax
import jax.numpy as jnp
from jax import lax
from jax.experimental import pallas as pl
from jax.experimental.pallas import tpu as pltpu
from jax.sharding import PartitionSpec as P

MESH = pl.DeviceIdType.MESH
F32 = jnp.float32
BF16 = jnp.bfloat16
PIECES = 4
SUBS = 1
UNROLL = 32


def kernel(
    num_inst, num_tp, q_hbm, k_hbm, v_hbm, w_hbm, len_hbm, table_hbm, route_hbm, out_ref,
    len_ref, table_ref, route_ref, k_buf, v_buf, w_buf, q_in, q_heads, score, mixed, act, place_rows, rs_send, rs_in, own, gathered, y_send,
    int_sem, k_sem, v_sem, w_sem, q_own_sem, q_ssem, q_rsem, rs_ssem, rs_rsem, ag_ssem, ag_rsem, y_ssem, y_rsem,
):
    me = lax.axis_index("inst")
    tp = lax.axis_index("tp")
    blocks, kv_heads, block_len, head_dim = k_buf.shape
    cap = q_in.shape[1]
    cols = q_in.shape[2]
    rows = route_ref.shape[1]
    heads = cols // head_dim
    group = heads // kv_heads
    per_req = table_ref.shape[1] // rows
    sub = w_buf.shape[3]
    chunk = SUBS * sub

    def inst_peer(k):
        return lax.rem(me + k, num_inst)

    def tp_peer(k):
        return lax.rem(tp + k, num_tp)

    size = blocks // PIECES
    k_copies = [
        pltpu.make_async_copy(k_hbm.at[pl.ds(i * size, size)], k_buf.at[pl.ds(i * size, size)], k_sem.at[i])
        for i in range(PIECES)
    ]
    v_copies = [
        pltpu.make_async_copy(v_hbm.at[pl.ds(i * size, size)], v_buf.at[pl.ds(i * size, size)], v_sem.at[i])
        for i in range(PIECES)
    ]
    w_copies = []
    for s in range(SUBS):
        for i in range(num_tp):
            column = pl.multiple_of(tp_peer((i + 1) % num_tp) * chunk + s * sub, 128)
            w_copies.append(
                pltpu.make_async_copy(w_hbm.at[:, pl.ds(column, sub)], w_buf.at[s, i], w_sem.at[s * num_tp + i])
            )
    route_copy = pltpu.make_async_copy(route_hbm, route_ref, int_sem.at[0])
    len_copy = pltpu.make_async_copy(len_hbm, len_ref, int_sem.at[1])
    table_copy = pltpu.make_async_copy(table_hbm, table_ref, int_sem.at[2])
    q_own = pltpu.make_async_copy(q_hbm.at[me], q_in.at[me], q_own_sem)
    for c in [route_copy, len_copy, table_copy, q_own] + k_copies + v_copies + w_copies:
        c.start()

    barrier = pltpu.get_barrier_semaphore()
    for k in range(1, num_inst):
        pl.semaphore_signal(barrier, inc=1, device_id={"inst": inst_peer(k)}, device_id_type=MESH)
    for k in range(1, num_tp):
        pl.semaphore_signal(barrier, inc=1, device_id={"tp": tp_peer(k)}, device_id_type=MESH)
    pl.semaphore_wait(barrier, num_inst + num_tp - 2)

    q_copies = []
    for k in range(1, num_inst):
        peer = inst_peer(k)
        c = pltpu.make_async_remote_copy(
            src_ref=q_hbm.at[peer], dst_ref=q_in.at[me], send_sem=q_ssem.at[k], recv_sem=q_rsem.at[me],
            device_id={"inst": peer}, device_id_type=MESH,
        )
        c.start()
        q_copies.append(c)

    route_copy.wait()
    target = route_ref[...]
    line = lax.broadcasted_iota(jnp.int32, (128, rows), 0)
    onehot = (target == line).astype(F32)
    earlier = (
        lax.broadcasted_iota(jnp.int32, (rows, rows), 0) < lax.broadcasted_iota(jnp.int32, (rows, rows), 1)
    ).astype(F32)
    before = jnp.dot(onehot, earlier, preferred_element_type=F32)
    rank = jnp.sum(before * onehot, axis=0, keepdims=True).astype(jnp.int32)
    turned = (target * cap + rank == line).astype(F32)
    place_rows[...] = turned[:num_inst * cap, :].astype(BF16)
    lane = lax.broadcasted_iota(jnp.int32, (rows, 128), 1).astype(F32)
    slot = jnp.sum(jnp.transpose(turned) * lane, axis=1, keepdims=True).astype(jnp.int32)

    q_own.wait()
    for k in range(1, num_inst):
        src = inst_peer(k)
        pltpu.make_async_remote_copy(
            src_ref=q_hbm.at[src], dst_ref=q_in.at[src], send_sem=q_ssem.at[k], recv_sem=q_rsem.at[src],
            device_id={"inst": src}, device_id_type=MESH,
        ).wait_recv()
    total = jnp.zeros((rows, cols), F32)
    for t in range(num_inst):
        here = (slot - t * cap == lax.broadcasted_iota(jnp.int32, (rows, cap), 1)).astype(F32).astype(BF16)
        total = total + jnp.dot(here, q_in[t], preferred_element_type=F32)
    for h in range(heads):
        q_heads[:, h, :] = total[:, h * head_dim:(h + 1) * head_dim]

    len_copy.wait()
    table_copy.wait()
    for c in k_copies:
        c.wait()
    span = per_req * block_len
    position = lax.broadcasted_iota(jnp.int32, (group, span), 1)
    scale = 1.0 / math.sqrt(head_dim)

    def score_step(i, carry):
        for u in range(UNROLL):
            r = i * UNROLL + u
            limit = len_ref[0, r]
            ids = [table_ref[0, r * per_req + m] for m in range(per_req)]
            for j in range(kv_heads):
                query = q_heads[r, pl.ds(j * group, group), :].astype(BF16)
                keys = jnp.concatenate([k_buf[b, j] for b in ids], axis=0)
                s = lax.dot_general(query, keys, (((1,), (1,)), ((), ())), preferred_element_type=F32) * scale
                score[r, pl.ds(j * group, group), :] = jnp.where(position < limit, s, -1e30)
        return carry

    lax.fori_loop(0, rows // UNROLL, score_step, 0)

    def soft_step(i, carry):
        x = score[pl.ds(i * UNROLL, UNROLL)]
        e = jnp.exp(x - jnp.max(x, axis=2, keepdims=True))
        score[pl.ds(i * UNROLL, UNROLL)] = e * (1.0 / jnp.sum(e, axis=2, keepdims=True))
        return carry

    lax.fori_loop(0, rows // UNROLL, soft_step, 0)

    for c in v_copies:
        c.wait()

    def mix_step(i, carry):
        for u in range(UNROLL):
            r = i * UNROLL + u
            ids = [table_ref[0, r * per_req + m] for m in range(per_req)]
            for j in range(kv_heads):
                weight = score[r, pl.ds(j * group, group), :].astype(BF16)
                values = jnp.concatenate([v_buf[b, j] for b in ids], axis=0)
                mixed[r, pl.ds(j * group, group), :] = jnp.dot(weight, values, preferred_element_type=F32)
        return carry

    lax.fori_loop(0, rows // UNROLL, mix_step, 0)
    for h in range(heads):
        act[:, h * head_dim:(h + 1) * head_dim] = mixed[:, h, :].astype(BF16)

    tile = min(256, sub)
    rs_copies, ag_copies, y_copies = [], [], []
    for s in range(SUBS):
        for i in range(num_tp):
            w_copies[s * num_tp + i].wait()
            for n in range(0, sub, tile):
                part = jnp.dot(act[...], w_buf[s, i, :, n:n + tile], preferred_element_type=F32)
                if i < num_tp - 1:
                    rs_send[s, i, :, n:n + tile] = part.astype(BF16)
                else:
                    own[s, :, n:n + tile] = part
            if i < num_tp - 1:
                c = pltpu.make_async_remote_copy(
                    src_ref=rs_send.at[s, i], dst_ref=rs_in.at[s, tp],
                    send_sem=rs_ssem.at[s, i], recv_sem=rs_rsem.at[s, tp],
                    device_id={"tp": tp_peer(i + 1)}, device_id_type=MESH,
                )
                c.start()
                rs_copies.append(c)

    def columns_of(s, owner):
        return pl.ds(pl.multiple_of(owner * chunk + s * sub, 128), sub)

    def move(s, k):
        owner = tp_peer(k)
        spread = jnp.dot(place_rows[...], gathered[s, owner], preferred_element_type=F32)
        for t in range(num_inst):
            y_send[s, k, t] = spread[t * cap:(t + 1) * cap].astype(BF16)
        for n in list(range(1, num_inst)) + [0]:
            dst = inst_peer(n)
            if n == 0:
                out_ref[me, :, columns_of(s, owner)] = y_send[s, k, me]
                continue
            c = pltpu.make_async_remote_copy(
                src_ref=y_send.at[s, k, dst], dst_ref=out_ref.at[me, :, columns_of(s, owner)],
                send_sem=y_ssem.at[s * num_tp + k, n], recv_sem=y_rsem.at[s * num_tp + owner, me],
                device_id={"inst": dst}, device_id_type=MESH,
            )
            c.start()
            y_copies.append(c)

    for s in range(SUBS):
        summed = own[s]
        for k in range(1, num_tp):
            src = tp_peer(k)
            pltpu.make_async_remote_copy(
                src_ref=rs_send.at[s, 0], dst_ref=rs_in.at[s, src],
                send_sem=rs_ssem.at[s, 0], recv_sem=rs_rsem.at[s, src],
                device_id={"tp": src}, device_id_type=MESH,
            ).wait_recv()
            summed = summed + rs_in[s, src].astype(F32)
        gathered[s, tp] = summed.astype(BF16)
        for k in range(1, num_tp):
            c = pltpu.make_async_remote_copy(
                src_ref=gathered.at[s, tp], dst_ref=gathered.at[s, tp],
                send_sem=ag_ssem.at[s, k], recv_sem=ag_rsem.at[s, tp],
                device_id={"tp": tp_peer(k)}, device_id_type=MESH,
            )
            c.start()
            ag_copies.append(c)
        move(s, 0)

    for s in range(SUBS):
        for k in range(1, num_tp):
            src = tp_peer(k)
            pltpu.make_async_remote_copy(
                src_ref=gathered.at[s, src], dst_ref=gathered.at[s, src],
                send_sem=ag_ssem.at[s, k], recv_sem=ag_rsem.at[s, src],
                device_id={"tp": src}, device_id_type=MESH,
            ).wait_recv()
            move(s, k)

    for s in range(SUBS):
        for k in range(num_tp):
            owner = tp_peer(k)
            for n in range(1, num_inst):
                src = inst_peer(n)
                pltpu.make_async_remote_copy(
                    src_ref=y_send.at[s, k, n], dst_ref=out_ref.at[src, :, columns_of(s, owner)],
                    send_sem=y_ssem.at[s * num_tp + k, n], recv_sem=y_rsem.at[s * num_tp + owner, src],
                    device_id={"inst": src}, device_id_type=MESH,
                ).wait_recv()
    for c in q_copies + rs_copies + ag_copies + y_copies:
        c.wait_send()


def local(queries, k_pool, v_pool, out_weight, lengths, block_table, routes):
    num_inst = lax.axis_size("inst")
    num_tp = lax.axis_size("tp")
    slots, cols = queries.shape
    cap = slots // num_inst
    blocks, kv_heads, block_len, head_dim = k_pool.shape
    rows = routes.shape[0]
    features = out_weight.shape[1]
    sub = features // num_tp // SUBS
    heads = cols // head_dim
    span = block_table.shape[1] // rows * block_len
    hbm = pl.BlockSpec(memory_space=pltpu.HBM)
    vmem = pl.BlockSpec(memory_space=pltpu.VMEM)
    dma = pltpu.SemaphoreType.DMA
    out = pl.pallas_call(
        functools.partial(kernel, num_inst, num_tp),
        out_shape=jax.ShapeDtypeStruct((num_inst, cap, features), BF16),
        in_specs=[hbm] * 7,
        out_specs=vmem,
        scratch_shapes=[
            pltpu.SMEM(lengths.shape, jnp.int32),
            pltpu.SMEM(block_table.shape, jnp.int32),
            pltpu.VMEM((1, rows), jnp.int32),
            pltpu.VMEM(k_pool.shape, BF16),
            pltpu.VMEM(v_pool.shape, BF16),
            pltpu.VMEM((SUBS, num_tp, cols, sub), BF16),
            pltpu.VMEM((num_inst, cap, cols), BF16),
            pltpu.VMEM((rows, heads, head_dim), F32),
            pltpu.VMEM((rows, heads, span), F32),
            pltpu.VMEM((rows, heads, head_dim), F32),
            pltpu.VMEM((rows, cols), BF16),
            pltpu.VMEM((num_inst * cap, rows), BF16),
            pltpu.VMEM((SUBS, num_tp, rows, sub), BF16),
            pltpu.VMEM((SUBS, num_tp, rows, sub), BF16),
            pltpu.VMEM((SUBS, rows, sub), F32),
            pltpu.VMEM((SUBS, num_tp, rows, sub), BF16),
            pltpu.VMEM((SUBS, num_tp, num_inst, cap, sub), BF16),
            dma((3,)),
            dma((PIECES,)),
            dma((PIECES,)),
            dma((SUBS * num_tp,)),
            dma,
            dma((num_inst,)),
            dma((num_inst,)),
            dma((SUBS, num_tp)),
            dma((SUBS, num_tp)),
            dma((SUBS, num_tp)),
            dma((SUBS, num_tp)),
            dma((SUBS * num_tp, num_inst)),
            dma((SUBS * num_tp, num_inst)),
        ],
        compiler_params=pltpu.CompilerParams(
            collective_id=0, has_side_effects=True, vmem_limit_bytes=64 * 1024 * 1024 - 65536
        ),
        cost_estimate=pl.CostEstimate(flops=10**9, bytes_accessed=33 * 10**6, transcendentals=300000),
    )(queries.reshape(num_inst, cap, cols), k_pool, v_pool, out_weight, lengths, block_table, routes.reshape(1, rows))
    return out.reshape(slots, features)


def solution(mesh):
    return jax.shard_map(
        local,
        mesh=mesh,
        in_specs=(
            P(("groups", "inst"), "tp"),
            P(("groups", "inst"), "tp", None, None),
            P(("groups", "inst"), "tp", None, None),
            P("tp", None),
            P(("groups", "inst"), None),
            P(("groups", "inst"), None),
            P(("groups", "inst"), None),
        ),
        out_specs=P(("groups", "inst"), None),
        check_vma=False,
    )
```

```python
import functools
import math

import jax
import jax.numpy as jnp
from jax import lax
from jax.experimental import pallas as pl
from jax.experimental.pallas import tpu as pltpu
from jax.sharding import PartitionSpec as P

MESH = pl.DeviceIdType.MESH
F32 = jnp.float32
BF16 = jnp.bfloat16
PIECES = 4
SUBS = 1
UNROLL = 32


def kernel(
    num_inst, num_tp, q_hbm, k_hbm, v_hbm, w_hbm, len_hbm, table_hbm, route_hbm, out_ref,
    len_ref, table_ref, route_ref, k_buf, v_buf, w_buf, q_in, q_heads, score, mixed, act, place_rows, rs_send, rs_in, own, gathered, y_send,
    int_sem, k_sem, v_sem, w_sem, q_own_sem, q_ssem, q_rsem, rs_ssem, rs_rsem, ag_ssem, ag_rsem, y_ssem, y_rsem,
):
    me = lax.axis_index("inst")
    tp = lax.axis_index("tp")
    blocks, kv_heads, block_len, head_dim = k_buf.shape
    cap = q_in.shape[1]
    cols = q_in.shape[2]
    rows = route_ref.shape[1]
    heads = cols // head_dim
    group = heads // kv_heads
    per_req = table_ref.shape[1] // rows
    sub = w_buf.shape[3]
    chunk = SUBS * sub

    def inst_peer(k):
        return lax.rem(me + k, num_inst)

    def tp_peer(k):
        return lax.rem(tp + k, num_tp)

    size = blocks // PIECES
    k_copies = [
        pltpu.make_async_copy(k_hbm.at[pl.ds(i * size, size)], k_buf.at[pl.ds(i * size, size)], k_sem.at[i])
        for i in range(PIECES)
    ]
    v_copies = [
        pltpu.make_async_copy(v_hbm.at[pl.ds(i * size, size)], v_buf.at[pl.ds(i * size, size)], v_sem.at[i])
        for i in range(PIECES)
    ]
    w_copies = []
    for s in range(SUBS):
        for i in range(num_tp):
            column = pl.multiple_of(tp_peer((i + 1) % num_tp) * chunk + s * sub, 128)
            w_copies.append(
                pltpu.make_async_copy(w_hbm.at[:, pl.ds(column, sub)], w_buf.at[s, i], w_sem.at[s * num_tp + i])
            )
    route_copy = pltpu.make_async_copy(route_hbm, route_ref, int_sem.at[0])
    len_copy = pltpu.make_async_copy(len_hbm, len_ref, int_sem.at[1])
    table_copy = pltpu.make_async_copy(table_hbm, table_ref, int_sem.at[2])
    q_own = pltpu.make_async_copy(q_hbm.at[me], q_in.at[me], q_own_sem)
    for c in [route_copy, len_copy, table_copy, q_own] + k_copies + v_copies:
        c.start()

    barrier = pltpu.get_barrier_semaphore()
    for k in range(1, num_inst):
        pl.semaphore_signal(barrier, inc=1, device_id={"inst": inst_peer(k)}, device_id_type=MESH)
    for k in range(1, num_tp):
        pl.semaphore_signal(barrier, inc=1, device_id={"tp": tp_peer(k)}, device_id_type=MESH)
    pl.semaphore_wait(barrier, num_inst + num_tp - 2)

    q_copies = []
    for k in range(1, num_inst):
        peer = inst_peer(k)
        c = pltpu.make_async_remote_copy(
            src_ref=q_hbm.at[peer], dst_ref=q_in.at[me], send_sem=q_ssem.at[k], recv_sem=q_rsem.at[me],
            device_id={"inst": peer}, device_id_type=MESH,
        )
        c.start()
        q_copies.append(c)

    route_copy.wait()
    target = route_ref[...]
    line = lax.broadcasted_iota(jnp.int32, (128, rows), 0)
    onehot = (target == line).astype(F32)
    earlier = (
        lax.broadcasted_iota(jnp.int32, (rows, rows), 0) < lax.broadcasted_iota(jnp.int32, (rows, rows), 1)
    ).astype(F32)
    before = jnp.dot(onehot, earlier, preferred_element_type=F32)
    rank = jnp.sum(before * onehot, axis=0, keepdims=True).astype(jnp.int32)
    turned = (target * cap + rank == line).astype(F32)
    place_rows[...] = turned[:num_inst * cap, :].astype(BF16)
    lane = lax.broadcasted_iota(jnp.int32, (rows, 128), 1).astype(F32)
    slot = jnp.sum(jnp.transpose(turned) * lane, axis=1, keepdims=True).astype(jnp.int32)

    q_own.wait()
    for k in range(1, num_inst):
        src = inst_peer(k)
        pltpu.make_async_remote_copy(
            src_ref=q_hbm.at[src], dst_ref=q_in.at[src], send_sem=q_ssem.at[k], recv_sem=q_rsem.at[src],
            device_id={"inst": src}, device_id_type=MESH,
        ).wait_recv()
    total = jnp.zeros((rows, cols), F32)
    for t in range(num_inst):
        here = (slot - t * cap == lax.broadcasted_iota(jnp.int32, (rows, cap), 1)).astype(F32).astype(BF16)
        total = total + jnp.dot(here, q_in[t], preferred_element_type=F32)
    for h in range(heads):
        q_heads[:, h, :] = total[:, h * head_dim:(h + 1) * head_dim]

    len_copy.wait()
    table_copy.wait()
    for c in k_copies:
        c.wait()
    for c in w_copies:
        c.start()
    span = per_req * block_len
    position = lax.broadcasted_iota(jnp.int32, (group, span), 1)
    scale = 1.0 / math.sqrt(head_dim)

    def score_step(i, carry):
        for u in range(UNROLL):
            r = i * UNROLL + u
            limit = len_ref[0, r]
            ids = [table_ref[0, r * per_req + m] for m in range(per_req)]
            for j in range(kv_heads):
                query = q_heads[r, pl.ds(j * group, group), :].astype(BF16)
                keys = jnp.concatenate([k_buf[b, j] for b in ids], axis=0)
                s = lax.dot_general(query, keys, (((1,), (1,)), ((), ())), preferred_element_type=F32) * scale
                score[r, pl.ds(j * group, group), :] = jnp.where(position < limit, s, -1e30)
        return carry

    lax.fori_loop(0, rows // UNROLL, score_step, 0)

    def soft_step(i, carry):
        x = score[pl.ds(i * UNROLL, UNROLL)]
        e = jnp.exp(x - jnp.max(x, axis=2, keepdims=True))
        score[pl.ds(i * UNROLL, UNROLL)] = e * (1.0 / jnp.sum(e, axis=2, keepdims=True))
        return carry

    lax.fori_loop(0, rows // UNROLL, soft_step, 0)

    for c in v_copies:
        c.wait()

    def mix_step(i, carry):
        for u in range(UNROLL):
            r = i * UNROLL + u
            ids = [table_ref[0, r * per_req + m] for m in range(per_req)]
            for j in range(kv_heads):
                weight = score[r, pl.ds(j * group, group), :].astype(BF16)
                values = jnp.concatenate([v_buf[b, j] for b in ids], axis=0)
                mixed[r, pl.ds(j * group, group), :] = jnp.dot(weight, values, preferred_element_type=F32)
        return carry

    lax.fori_loop(0, rows // UNROLL, mix_step, 0)
    for h in range(heads):
        act[:, h * head_dim:(h + 1) * head_dim] = mixed[:, h, :].astype(BF16)

    tile = min(256, sub)
    rs_copies, ag_copies, y_copies = [], [], []
    for s in range(SUBS):
        for i in range(num_tp):
            w_copies[s * num_tp + i].wait()
            for n in range(0, sub, tile):
                part = jnp.dot(act[...], w_buf[s, i, :, n:n + tile], preferred_element_type=F32)
                if i < num_tp - 1:
                    rs_send[s, i, :, n:n + tile] = part.astype(BF16)
                else:
                    own[s, :, n:n + tile] = part
            if i < num_tp - 1:
                c = pltpu.make_async_remote_copy(
                    src_ref=rs_send.at[s, i], dst_ref=rs_in.at[s, tp],
                    send_sem=rs_ssem.at[s, i], recv_sem=rs_rsem.at[s, tp],
                    device_id={"tp": tp_peer(i + 1)}, device_id_type=MESH,
                )
                c.start()
                rs_copies.append(c)

    def columns_of(s, owner):
        return pl.ds(pl.multiple_of(owner * chunk + s * sub, 128), sub)

    def move(s, k):
        owner = tp_peer(k)
        spread = jnp.dot(place_rows[...], gathered[s, owner], preferred_element_type=F32)
        for t in range(num_inst):
            y_send[s, k, t] = spread[t * cap:(t + 1) * cap].astype(BF16)
        for n in list(range(1, num_inst)) + [0]:
            dst = inst_peer(n)
            if n == 0:
                out_ref[me, :, columns_of(s, owner)] = y_send[s, k, me]
                continue
            c = pltpu.make_async_remote_copy(
                src_ref=y_send.at[s, k, dst], dst_ref=out_ref.at[me, :, columns_of(s, owner)],
                send_sem=y_ssem.at[s * num_tp + k, n], recv_sem=y_rsem.at[s * num_tp + owner, me],
                device_id={"inst": dst}, device_id_type=MESH,
            )
            c.start()
            y_copies.append(c)

    for s in range(SUBS):
        summed = own[s]
        for k in range(1, num_tp):
            src = tp_peer(k)
            pltpu.make_async_remote_copy(
                src_ref=rs_send.at[s, 0], dst_ref=rs_in.at[s, src],
                send_sem=rs_ssem.at[s, 0], recv_sem=rs_rsem.at[s, src],
                device_id={"tp": src}, device_id_type=MESH,
            ).wait_recv()
            summed = summed + rs_in[s, src].astype(F32)
        gathered[s, tp] = summed.astype(BF16)
        for k in range(1, num_tp):
            c = pltpu.make_async_remote_copy(
                src_ref=gathered.at[s, tp], dst_ref=gathered.at[s, tp],
                send_sem=ag_ssem.at[s, k], recv_sem=ag_rsem.at[s, tp],
                device_id={"tp": tp_peer(k)}, device_id_type=MESH,
            )
            c.start()
            ag_copies.append(c)
        move(s, 0)

    for s in range(SUBS):
        for k in range(1, num_tp):
            src = tp_peer(k)
            pltpu.make_async_remote_copy(
                src_ref=gathered.at[s, src], dst_ref=gathered.at[s, src],
                send_sem=ag_ssem.at[s, k], recv_sem=ag_rsem.at[s, src],
                device_id={"tp": src}, device_id_type=MESH,
            ).wait_recv()
            move(s, k)

    for s in range(SUBS):
        for k in range(num_tp):
            owner = tp_peer(k)
            for n in range(1, num_inst):
                src = inst_peer(n)
                pltpu.make_async_remote_copy(
                    src_ref=y_send.at[s, k, n], dst_ref=out_ref.at[src, :, columns_of(s, owner)],
                    send_sem=y_ssem.at[s * num_tp + k, n], recv_sem=y_rsem.at[s * num_tp + owner, src],
                    device_id={"inst": src}, device_id_type=MESH,
                ).wait_recv()
    for c in q_copies + rs_copies + ag_copies + y_copies:
        c.wait_send()


def local(queries, k_pool, v_pool, out_weight, lengths, block_table, routes):
    num_inst = lax.axis_size("inst")
    num_tp = lax.axis_size("tp")
    slots, cols = queries.shape
    cap = slots // num_inst
    blocks, kv_heads, block_len, head_dim = k_pool.shape
    rows = routes.shape[0]
    features = out_weight.shape[1]
    sub = features // num_tp // SUBS
    heads = cols // head_dim
    span = block_table.shape[1] // rows * block_len
    hbm = pl.BlockSpec(memory_space=pltpu.HBM)
    vmem = pl.BlockSpec(memory_space=pltpu.VMEM)
    dma = pltpu.SemaphoreType.DMA
    out = pl.pallas_call(
        functools.partial(kernel, num_inst, num_tp),
        out_shape=jax.ShapeDtypeStruct((num_inst, cap, features), BF16),
        in_specs=[hbm] * 7,
        out_specs=vmem,
        scratch_shapes=[
            pltpu.SMEM(lengths.shape, jnp.int32),
            pltpu.SMEM(block_table.shape, jnp.int32),
            pltpu.VMEM((1, rows), jnp.int32),
            pltpu.VMEM(k_pool.shape, BF16),
            pltpu.VMEM(v_pool.shape, BF16),
            pltpu.VMEM((SUBS, num_tp, cols, sub), BF16),
            pltpu.VMEM((num_inst, cap, cols), BF16),
            pltpu.VMEM((rows, heads, head_dim), F32),
            pltpu.VMEM((rows, heads, span), F32),
            pltpu.VMEM((rows, heads, head_dim), F32),
            pltpu.VMEM((rows, cols), BF16),
            pltpu.VMEM((num_inst * cap, rows), BF16),
            pltpu.VMEM((SUBS, num_tp, rows, sub), BF16),
            pltpu.VMEM((SUBS, num_tp, rows, sub), BF16),
            pltpu.VMEM((SUBS, rows, sub), F32),
            pltpu.VMEM((SUBS, num_tp, rows, sub), BF16),
            pltpu.VMEM((SUBS, num_tp, num_inst, cap, sub), BF16),
            dma((3,)),
            dma((PIECES,)),
            dma((PIECES,)),
            dma((SUBS * num_tp,)),
            dma,
            dma((num_inst,)),
            dma((num_inst,)),
            dma((SUBS, num_tp)),
            dma((SUBS, num_tp)),
            dma((SUBS, num_tp)),
            dma((SUBS, num_tp)),
            dma((SUBS * num_tp, num_inst)),
            dma((SUBS * num_tp, num_inst)),
        ],
        compiler_params=pltpu.CompilerParams(
            collective_id=0, has_side_effects=True, vmem_limit_bytes=64 * 1024 * 1024 - 65536
        ),
        cost_estimate=pl.CostEstimate(flops=10**9, bytes_accessed=33 * 10**6, transcendentals=300000),
    )(queries.reshape(num_inst, cap, cols), k_pool, v_pool, out_weight, lengths, block_table, routes.reshape(1, rows))
    return out.reshape(slots, features)


def solution(mesh):
    return jax.shard_map(
        local,
        mesh=mesh,
        in_specs=(
            P(("groups", "inst"), "tp"),
            P(("groups", "inst"), "tp", None, None),
            P(("groups", "inst"), "tp", None, None),
            P("tp", None),
            P(("groups", "inst"), None),
            P(("groups", "inst"), None),
            P(("groups", "inst"), None),
        ),
        out_specs=P(("groups", "inst"), None),
        check_vma=False,
    )
```
